512 devices in a mesh: dp: 64 (over x_hi, z, core), tensor: 8 (over y, x_lo).
Axes of the slice: x: 4 (x_hi: 2, x_lo: 2; x = x_hi * 2 + x_lo), y: 4, z: 16, core: 2. Of those that a mesh axis runs over, the one named last changes fastest.
Arguments:
- grad_hidden: bfloat16 [1024, 16384], P('dp', 'tensor'), may hold values from -8 to 8
- gate_in: bfloat16 [1024, 16384], P('dp', 'tensor'), may hold values from -8 to 8
- up_in: bfloat16 [1024, 16384], P('dp', 'tensor'), may hold values from -6 to 6
- gate_weight: bfloat16 [8192, 16384], P('dp', 'tensor'), may hold values from -0.046875 to 0.046875
- up_weight: bfloat16 [8192, 16384], P('dp', 'tensor'), may hold values from -0.046875 to 0.046875
- prior_factor: bfloat16 [16384, 16384], P('tensor', 'dp'), may hold values from -1.1953125 to 1.1953125
Outputs:
- input_grad: bfloat16 [1024, 8192], P(None, 'dp')
- factor: float32 [16384, 16384], P('tensor', 'dp')
The draws below stay inside these ranges and needn't reach their ends.
All inputs are finite; a program needn't handle non-finite values.
Results may differ from the reference program's by a relative error of at most 0.0049.
Values may be sent and summed in bfloat16 or wider, within the bound.
No kernel may reach another device: no remote copies, remote signals or barrier semaphores. Data moves between devices by JAX's collectives and lax.ppermute only.
A program may use at most 64 MiB of HBM per device.

```python
import jax
import jax.numpy as jnp
from jax import lax

D = 8192
FFW = 16384
TOKENS = 1024


def level_of(key, extent, split, least, largest):
    loudness = 1.0
    for dim, parts in split:
        steps = jax.random.uniform(jax.random.fold_in(jax.random.fold_in(key, 6), dim), (parts,), jnp.float32, least / len(split), largest / len(split))
        loudness = loudness * jnp.repeat(jnp.exp(steps), extent[dim] // parts).reshape((-1,) + (1,) * (len(extent) - 1 - dim))
    return loudness


def centred(key, extent, spread, bound, cuts=(), dtype=jnp.bfloat16):
    factor_of = level_of(key, extent, cuts, -0.22, 0.18) if cuts else 1.0
    array = jax.random.normal(key, extent, jnp.float32) * spread * factor_of
    return jnp.minimum(jnp.maximum(array, -bound), bound).astype(dtype)


def setup_inputs(seed: int = 0) -> dict:
    seeds = jax.random.split(jax.random.key(seed), 7)
    grad_hidden = centred(seeds[0], (TOKENS, FFW), 2.0, 8.0, ((0, 64), (1, 8)))
    gate_in = centred(seeds[1], (TOKENS, FFW), 2.0, 8.0, ((0, 64), (1, 8)))
    up_in = centred(seeds[2], (TOKENS, FFW), 1.0, 6.0, ((0, 64), (1, 8)))
    gate_weight = centred(seeds[3], (D, FFW), FFW ** -0.5, 0.046875, ((0, 64), (1, 8)))
    up_weight = centred(seeds[4], (D, FFW), FFW ** -0.5, 0.046875, ((0, 64), (1, 8)))
    prior_factor = centred(seeds[5], (FFW, FFW), 0.2, 1.1953125, ((0, 8), (1, 64)))
    return dict(grad_hidden=grad_hidden, gate_in=gate_in, up_in=up_in, gate_weight=gate_weight, up_weight=up_weight, prior_factor=prior_factor)


def reference(grad_hidden, gate_in, up_in, gate_weight, up_weight, prior_factor):
    gate_val = gate_in.astype(jnp.float32)
    upper_val = up_in.astype(jnp.float32)
    incoming = grad_hidden.astype(jnp.float32)
    sigmoid_val = jax.nn.sigmoid(gate_val)
    gate_grad = (incoming * upper_val * sigmoid_val * (1.0 + gate_val * (1.0 - sigmoid_val))).astype(jnp.bfloat16)
    upper_grad = (incoming * gate_val * sigmoid_val).astype(jnp.bfloat16)
    first = jnp.dot(gate_grad, gate_weight.T, preferred_element_type=jnp.float32)
    second = jnp.dot(upper_grad, up_weight.T, preferred_element_type=jnp.float32)
    input_grad = (first + second).astype(jnp.bfloat16)
    gram = lax.dot_general(gate_grad, gate_grad, (((0,), (0,)), ((), ())), preferred_element_type=jnp.float32)
    factor = prior_factor.astype(jnp.float32) + gram / TOKENS
    return input_grad, factor
```

```python
import jax
import jax.numpy as jnp
from jax import lax
from jax.sharding import Mesh, PartitionSpec as P

PLANE = ("y", "xl")
LINE = ("z", "c")
STEPS = 15


def derivatives(incoming_raw, gate_raw, upper_raw):
    gate_val = gate_raw.astype(jnp.float32)
    upper_val = upper_raw.astype(jnp.float32)
    incoming = incoming_raw.astype(jnp.float32)
    sigmoid_val = jax.nn.sigmoid(gate_val)
    gate_grad = incoming * upper_val * sigmoid_val * (1.0 + gate_val * (1.0 - sigmoid_val))
    upper_grad = incoming * gate_val * sigmoid_val
    return (
        lax.reduce_precision(gate_grad, 8, 7),
        lax.reduce_precision(upper_grad, 8, 7),
    )


def pack(gate_grad, upper_grad):
    values = jnp.concatenate([gate_grad, upper_grad], axis=1)
    largest = jnp.max(jnp.abs(values), axis=1, keepdims=True)
    place = jnp.zeros_like(largest)
    scale = jnp.full_like(largest, 2.0**9)
    for step in range(1, STEPS):
        below = largest <= 2.0 ** (6 - 8 * step)
        place = jnp.where(below, float(step), place)
        scale = jnp.where(below, 2.0 ** (9 + 8 * step), scale)
    tail = jnp.broadcast_to(place, (values.shape[0], 128))
    return jnp.concatenate([values * scale, tail], axis=1).astype(jnp.float16)


def unpack(packed, width):
    place = packed[:, 2 * width : 2 * width + 1].astype(jnp.float32)
    undo = jnp.full_like(place, 2.0**-9)
    for step in range(1, STEPS):
        undo = jnp.where(place == float(step), 2.0 ** -(9 + 8 * step), undo)
    gate = (packed[:, :width].astype(jnp.float32) * undo).astype(jnp.bfloat16)
    upper = (packed[:, width : 2 * width].astype(jnp.float32) * undo).astype(jnp.bfloat16)
    return gate, upper


def shards(grad_hidden, gate_in, up_in, gate_weight, up_weight, prior_factor):
    width = grad_hidden.shape[1]
    block_width = prior_factor.shape[1]
    out_width = gate_weight.shape[0]
    n_tensor = lax.axis_size(PLANE)
    n_cross, n_line = lax.axis_size("xh"), lax.axis_size(LINE)
    rows = grad_hidden.shape[0]
    ratio = n_cross * n_line // n_tensor
    dp_index = lax.axis_index(("xh",) + LINE)

    packed = pack(*derivatives(grad_hidden, gate_in, up_in))
    packed = lax.all_gather(packed, "xh", axis=0, tiled=True)
    packed = lax.all_gather(packed, LINE, axis=0, tiled=True)
    gate_all, upper_all = unpack(packed, width)
    tokens_total = gate_all.shape[0]
    slot = tokens_total // n_tensor

    contract = (((1,), (1,)), ((), ()))
    partial_sum = lax.dot_general(
        gate_all, gate_weight, contract, preferred_element_type=jnp.float32
    ) + lax.dot_general(upper_all, up_weight, contract, preferred_element_type=jnp.float32)
    high = lax.reduce_precision(partial_sum, 8, 7)
    low = (partial_sum - high).astype(jnp.bfloat16)
    own_piece = lax.dynamic_slice_in_dim(gate_all, dp_index % ratio * block_width, block_width, 1)
    sent = jnp.concatenate([high.astype(jnp.bfloat16), low, own_piece], axis=1)
    sent = sent.reshape(n_tensor, slot, 2 * out_width + block_width)
    got = lax.all_to_all(sent, PLANE, 0, 0, tiled=True)
    sums = got[:, :, : 2 * out_width].astype(jnp.float32)
    total = jnp.sum(sums[:, :, :out_width] + sums[:, :, out_width:], axis=0)
    piece = lax.dynamic_index_in_dim(got, dp_index // ratio, 0, keepdims=False)[:, 2 * out_width :]
    share = jnp.concatenate([total.astype(jnp.bfloat16), piece], axis=1)
    everyone = lax.all_to_all(
        jnp.broadcast_to(share, (n_tensor,) + share.shape), PLANE, 0, 0, tiled=True
    ).reshape(tokens_total, out_width + block_width)
    input_grad = everyone[:, :out_width].reshape(n_line, n_cross, rows, out_width)
    input_grad = input_grad.transpose(1, 0, 2, 3).reshape(tokens_total, out_width)
    gram_tile = lax.dot_general(
        gate_all,
        everyone[:, out_width:],
        (((0,), (0,)), ((), ())),
        preferred_element_type=jnp.float32,
    )
    factor = prior_factor.astype(jnp.float32) + gram_tile / tokens_total
    return (input_grad, factor)


def solution(mesh):
    split = Mesh(mesh.devices.reshape(2, 16, 2, 4, 2), ("xh",) + LINE + PLANE)
    dp, tensor = ("xh",) + LINE, PLANE
    return jax.shard_map(
        shards,
        mesh=split,
        in_specs=(P(dp, tensor),) * 5 + (P(tensor, dp),),
        out_specs=(P(None, dp), P(tensor, dp)),
        check_vma=False,
    )
```

```python
import jax
import jax.numpy as jnp
from jax import lax
from jax.experimental.layout import Layout, with_layout_constraint
from jax.sharding import Mesh, PartitionSpec as P

PLANE = ("y", "xl")
LINE = ("z", "c")
STEPS = 15


def derivatives(incoming_raw, gate_raw, upper_raw):
    gate_val = gate_raw.astype(jnp.float32)
    upper_val = upper_raw.astype(jnp.float32)
    incoming = incoming_raw.astype(jnp.float32)
    sigmoid_val = jax.nn.sigmoid(gate_val)
    gate_grad = incoming * upper_val * sigmoid_val * (1.0 + gate_val * (1.0 - sigmoid_val))
    upper_grad = incoming * gate_val * sigmoid_val
    return (
        lax.reduce_precision(gate_grad, 8, 7),
        lax.reduce_precision(upper_grad, 8, 7),
    )


def pack(gate_grad, upper_grad):
    values = jnp.concatenate([gate_grad, upper_grad], axis=1)
    largest = jnp.max(jnp.abs(values), axis=1, keepdims=True)
    place = jnp.zeros_like(largest)
    scale = jnp.full_like(largest, 2.0**9)
    for step in range(1, STEPS):
        below = largest <= 2.0 ** (6 - 8 * step)
        place = jnp.where(below, float(step), place)
        scale = jnp.where(below, 2.0 ** (9 + 8 * step), scale)
    tail = jnp.broadcast_to(place, (values.shape[0], 128))
    return jnp.concatenate([values * scale, tail], axis=1).astype(jnp.float16)


def unpack(packed, width):
    place = packed[:, 2 * width : 2 * width + 1].astype(jnp.float32)
    undo = jnp.full_like(place, 2.0**-9)
    for step in range(1, STEPS):
        undo = jnp.where(place == float(step), 2.0 ** -(9 + 8 * step), undo)
    gate = (packed[:, :width].astype(jnp.float32) * undo).astype(jnp.bfloat16)
    upper = (packed[:, width : 2 * width].astype(jnp.float32) * undo).astype(jnp.bfloat16)
    return gate, upper


def by_rows(block):
    return with_layout_constraint(block, Layout(major_to_minor=(0, 1)))


def swap(block):
    return lax.ppermute(block, "xh", [(0, 1), (1, 0)])


def shards(grad_hidden, gate_in, up_in, gate_weight, up_weight, prior_factor):
    width = grad_hidden.shape[1]
    block_width = prior_factor.shape[1]
    out_width = gate_weight.shape[0]
    n_tensor, n_core = lax.axis_size(PLANE), lax.axis_size("c")
    cross, core, line = lax.axis_index("xh"), lax.axis_index("c"), lax.axis_index(LINE)
    ratio = width // block_width

    gate_both = jnp.concatenate([gate_weight, swap(gate_weight)])
    up_both = jnp.concatenate([up_weight, swap(up_weight)])
    packed = pack(*derivatives(grad_hidden, gate_in, up_in))
    packed = lax.all_gather(packed, LINE, axis=0, tiled=True)
    near_gate, near_upper = unpack(packed, width)
    near_gate, near_upper = by_rows(near_gate), by_rows(near_upper)
    rows = near_gate.shape[0]
    slot, half = rows // n_tensor, rows // n_core

    far_half = by_rows(swap(lax.dynamic_slice_in_dim(near_gate, core * half, half, 0)))
    far_other = by_rows(lax.ppermute(far_half, "c", [(0, 1), (1, 0)]))

    contract = (((1,), (1,)), ((), ()))
    partial_sum = lax.dot_general(
        near_gate, gate_both, contract, preferred_element_type=jnp.float32
    ) + lax.dot_general(near_upper, up_both, contract, preferred_element_type=jnp.float32)
    piece = lax.dynamic_slice_in_dim(near_gate, line % ratio * block_width, block_width, 1)
    sent = jnp.concatenate([partial_sum.astype(jnp.bfloat16), piece], axis=1)
    got = lax.all_to_all(
        sent.reshape(n_tensor, slot, 2 * out_width + block_width), PLANE, 0, 0, tiled=True
    )
    total = jnp.sum(got[:, :, : 2 * out_width].astype(jnp.float32), axis=0).astype(jnp.bfloat16)
    columns = got[:, :, 2 * out_width :]
    group, side = line // ratio, n_tensor // 2

    def share(which, sums):
        piece = lax.dynamic_index_in_dim(columns, which * side + group, 0, keepdims=False)
        return jnp.concatenate([sums, piece], axis=1)

    near = share(cross, total[:, :out_width])
    far = swap(share(1 - cross, total[:, out_width:]))
    both = jnp.stack([near, far])
    everyone = lax.all_to_all(
        jnp.broadcast_to(both, (n_tensor,) + both.shape), PLANE, 0, 0, tiled=True
    )
    near = everyone[:, 0].reshape(rows, out_width + block_width)
    far = everyone[:, 1].reshape(rows, out_width + block_width)
    far_cols = far[:, out_width:].reshape(n_core, half, block_width)

    def gram(tokens, columns):
        return lax.dot_general(
            tokens, columns, (((0,), (0,)), ((), ())), preferred_element_type=jnp.float32
        )

    gram_tile = (
        gram(near_gate, near[:, out_width:])
        + gram(far_half, lax.dynamic_index_in_dim(far_cols, core, 0, keepdims=False))
        + gram(far_other, lax.dynamic_index_in_dim(far_cols, 1 - core, 0, keepdims=False))
    )
    factor = prior_factor.astype(jnp.float32) + gram_tile / (2 * rows)
    first = jnp.where(cross == 0, near[:, :out_width], far[:, :out_width])
    second = jnp.where(cross == 0, far[:, :out_width], near[:, :out_width])
    return jnp.concatenate([first, second]), factor


def solution(mesh):
    split = Mesh(mesh.devices.reshape(2, 16, 2, 4, 2), ("xh",) + LINE + PLANE)
    dp, tensor = ("xh",) + LINE, PLANE
    return jax.shard_map(
        shards,
        mesh=split,
        in_specs=(P(dp, tensor),) * 5 + (P(tensor, dp),),
        out_specs=(P(None, dp), P(tensor, dp)),
        check_vma=False,
    )
```

```python
import jax
import jax.numpy as jnp
from jax import lax
from jax.experimental.layout import Layout, with_layout_constraint
from jax.sharding import Mesh, PartitionSpec as P

PLANE = ("y", "xl")
LINE = ("z", "c")
STEPS = 15


def derivatives(incoming_raw, gate_raw, upper_raw):
    gate_val = gate_raw.astype(jnp.float32)
    upper_val = upper_raw.astype(jnp.float32)
    incoming = incoming_raw.astype(jnp.float32)
    sigmoid_val = jax.nn.sigmoid(gate_val)
    gate_grad = incoming * upper_val * sigmoid_val * (1.0 + gate_val * (1.0 - sigmoid_val))
    upper_grad = incoming * gate_val * sigmoid_val
    return (
        lax.reduce_precision(gate_grad, 8, 7),
        lax.reduce_precision(upper_grad, 8, 7),
    )


def pack(gate_grad, upper_grad):
    values = jnp.concatenate([gate_grad, upper_grad], axis=1)
    largest = jnp.max(jnp.abs(values), axis=1, keepdims=True)
    place = jnp.zeros_like(largest)
    scale = jnp.full_like(largest, 2.0**9)
    for step in range(1, STEPS):
        below = largest <= 2.0 ** (6 - 8 * step)
        place = jnp.where(below, float(step), place)
        scale = jnp.where(below, 2.0 ** (9 + 8 * step), scale)
    tail = jnp.broadcast_to(place, (values.shape[0], 128))
    return jnp.concatenate([values * scale, tail], axis=1).astype(jnp.float16)


def unpack(packed, width):
    place = packed[:, 2 * width : 2 * width + 1].astype(jnp.float32)
    undo = jnp.full_like(place, 2.0**-9)
    for step in range(1, STEPS):
        undo = jnp.where(place == float(step), 2.0 ** -(9 + 8 * step), undo)
    gate = (packed[:, :width].astype(jnp.float32) * undo).astype(jnp.bfloat16)
    upper = (packed[:, width : 2 * width].astype(jnp.float32) * undo).astype(jnp.bfloat16)
    return gate, upper


def by_rows(block):
    return with_layout_constraint(block, Layout(major_to_minor=(0, 1)))


def swap(block):
    return lax.ppermute(block, "xh", [(0, 1), (1, 0)])


def shards(grad_hidden, gate_in, up_in, gate_weight, up_weight, prior_factor):
    width = grad_hidden.shape[1]
    block_width = prior_factor.shape[1]
    out_width = gate_weight.shape[0]
    n_tensor, n_core = lax.axis_size(PLANE), lax.axis_size("c")
    cross, core, line = lax.axis_index("xh"), lax.axis_index("c"), lax.axis_index(LINE)
    ratio = width // block_width

    gate_grad, upper_grad = derivatives(grad_hidden, gate_in, up_in)
    sides = lax.all_gather(gate_grad.astype(jnp.bfloat16), ("xh", "z"), axis=0, tiled=True)
    gate_weight, up_weight, _ = lax.optimization_barrier((gate_weight, up_weight, gate_grad))
    gate_both = jnp.concatenate([gate_weight, swap(gate_weight)])
    up_both = jnp.concatenate([up_weight, swap(up_weight)])
    packed = lax.all_gather(pack(gate_grad, upper_grad), LINE, axis=0, tiled=True)
    near_gate, near_upper = unpack(packed, width)
    near_gate, near_upper = lax.optimization_barrier((by_rows(near_gate), by_rows(near_upper)))
    rows = near_gate.shape[0]
    slot, half = rows // n_tensor, rows // n_core

    far_mine = by_rows(lax.dynamic_slice_in_dim(sides, (1 - cross) * half, half, 0))

    contract = (((1,), (1,)), ((), ()))
    partial_sum = lax.dot_general(
        near_gate, gate_both, contract, preferred_element_type=jnp.float32
    ) + lax.dot_general(near_upper, up_both, contract, preferred_element_type=jnp.float32)
    piece = lax.dynamic_slice_in_dim(near_gate, line % ratio * block_width, block_width, 1)
    sent = jnp.concatenate([partial_sum.astype(jnp.bfloat16), piece], axis=1)
    got = lax.all_to_all(
        sent.reshape(n_tensor, slot, 2 * out_width + block_width), PLANE, 0, 0, tiled=True
    )
    total = jnp.sum(got[:, :, : 2 * out_width].astype(jnp.float32), axis=0).astype(jnp.bfloat16)
    columns = got[:, :, 2 * out_width :]
    group, side = line // ratio, n_tensor // 2

    def share(which, sums):
        piece = lax.dynamic_index_in_dim(columns, which * side + group, 0, keepdims=False)
        return jnp.concatenate([sums, piece], axis=1)

    near = share(cross, total[:, :out_width])
    far = swap(share(1 - cross, total[:, out_width:]))
    far, far_mine = lax.optimization_barrier((far, far_mine))
    far_other = by_rows(lax.ppermute(far_mine, "c", [(0, 1), (1, 0)]))
    both = jnp.stack([near, far])
    everyone = lax.all_to_all(
        jnp.broadcast_to(both, (n_tensor,) + both.shape), PLANE, 0, 0, tiled=True
    )
    near = everyone[:, 0].reshape(rows, out_width + block_width)
    far = everyone[:, 1].reshape(rows, out_width + block_width)
    far_cols = far[:, out_width:].reshape(-1, n_core, grad_hidden.shape[0], block_width)

    def far_columns(core):
        return lax.dynamic_index_in_dim(far_cols, core, 1, keepdims=False).reshape(half, block_width)

    def gram(tokens, columns):
        return lax.dot_general(
            tokens, columns, (((0,), (0,)), ((), ())), preferred_element_type=jnp.float32
        )

    gram_tile = (
        gram(near_gate, near[:, out_width:])
        + gram(far_mine, far_columns(core))
        + gram(far_other, far_columns(1 - core))
    )
    factor = prior_factor.astype(jnp.float32) + gram_tile / (2 * rows)
    first = jnp.where(cross == 0, near[:, :out_width], far[:, :out_width])
    second = jnp.where(cross == 0, far[:, :out_width], near[:, :out_width])
    return jnp.concatenate([first, second]), factor


def solution(mesh):
    split = Mesh(mesh.devices.reshape(2, 16, 2, 4, 2), ("xh",) + LINE + PLANE)
    dp, tensor = ("xh",) + LINE, PLANE
    return jax.shard_map(
        shards,
        mesh=split,
        in_specs=(P(dp, tensor),) * 5 + (P(tensor, dp),),
        out_specs=(P(None, dp), P(tensor, dp)),
        check_vma=False,
    )
```

```python
import jax
import jax.numpy as jnp
from jax import lax
from jax.experimental.layout import Layout, with_layout_constraint
from jax.sharding import Mesh, PartitionSpec as P

PLANE = ("y", "xl")
LINE = ("z", "c")
STEPS = 15


def derivatives(incoming_raw, gate_raw, upper_raw):
    gate_val = gate_raw.astype(jnp.float32)
    upper_val = upper_raw.astype(jnp.float32)
    incoming = incoming_raw.astype(jnp.float32)
    sigmoid_val = jax.nn.sigmoid(gate_val)
    gate_grad = incoming * upper_val * sigmoid_val * (1.0 + gate_val * (1.0 - sigmoid_val))
    upper_grad = incoming * gate_val * sigmoid_val
    return (
        lax.reduce_precision(gate_grad, 8, 7),
        lax.reduce_precision(upper_grad, 8, 7),
    )


def ladder(values):
    largest = jnp.max(jnp.abs(values), axis=1, keepdims=True)
    place = jnp.zeros_like(largest)
    scale = jnp.full_like(largest, 2.0**9)
    for step in range(1, STEPS):
        below = largest <= 2.0 ** (6 - 8 * step)
        place = jnp.where(below, float(step), place)
        scale = jnp.where(below, 2.0 ** (9 + 8 * step), scale)
    return scale, place


def unladder(values, place):
    place = place.astype(jnp.float32)
    undo = jnp.full_like(place, 2.0**-9)
    for step in range(1, STEPS):
        undo = jnp.where(place == float(step), 2.0 ** -(9 + 8 * step), undo)
    return (values.astype(jnp.float32) * undo).astype(jnp.bfloat16)


def by_rows(block):
    return with_layout_constraint(block, Layout(major_to_minor=(0, 1)))


def swap(block):
    return lax.ppermute(block, "xh", [(0, 1), (1, 0)])


def product(tokens, weight):
    return lax.dot_general(
        tokens, weight, (((1,), (1,)), ((), ())), preferred_element_type=jnp.float32
    )


def shards(grad_hidden, gate_in, up_in, gate_weight, up_weight, prior_factor):
    held, width = grad_hidden.shape
    block_width = prior_factor.shape[1]
    out_width = gate_weight.shape[0]
    n_tensor = lax.axis_size(PLANE)
    dp_index = lax.axis_index(("xh",) + LINE)
    cross, ratio = lax.axis_index("xh"), width // block_width

    gate_grad, upper_grad = derivatives(grad_hidden, gate_in, up_in)
    far_grad = swap(gate_grad.astype(jnp.bfloat16))
    up_both = jnp.concatenate([up_weight, swap(up_weight)])
    far_grad = far_grad.astype(jnp.float32)
    scale, place = ladder(jnp.concatenate([gate_grad, upper_grad], axis=1))
    far_scale, far_place = ladder(far_grad)
    lanes = lax.broadcasted_iota(jnp.int32, (held, 128), 1)
    packed = jnp.concatenate(
        [gate_grad * scale, upper_grad * scale, far_grad * far_scale]
        + [jnp.where(lanes < 64, place, far_place)],
        axis=1,
    ).astype(jnp.float16)
    packed = lax.all_gather(packed, LINE, axis=0, tiled=True)
    place, far_place = packed[:, 3 * width : 3 * width + 1], packed[:, -1:]
    upper_near = unladder(packed[:, width : 2 * width], place)
    gate_near = by_rows(unladder(packed[:, :width], place))
    gate_far = by_rows(unladder(packed[:, 2 * width : 3 * width], far_place))
    upper_near, gate_near, gate_far = lax.optimization_barrier((upper_near, gate_near, gate_far))
    rows = gate_near.shape[0]
    slot = rows // n_tensor

    upper_sum = product(upper_near, up_both)
    far_sum = swap(upper_sum[:, out_width:].astype(jnp.bfloat16)).astype(jnp.float32)

    def part(gate, upper_sum):
        sums = (product(gate, gate_weight) + upper_sum).astype(jnp.bfloat16)
        cut = lax.dynamic_slice_in_dim(gate, dp_index % ratio * block_width, block_width, 1)
        return jnp.concatenate([sums, cut], axis=1).reshape(n_tensor, 1, slot, -1)

    sent = jnp.concatenate(
        [part(gate_near, upper_sum[:, :out_width]), part(gate_far, far_sum)], axis=1
    )
    got = lax.all_to_all(sent, PLANE, 0, 0, tiled=True)
    total = jnp.sum(got[..., :out_width].astype(jnp.float32), axis=0).astype(jnp.bfloat16)
    piece = lax.dynamic_index_in_dim(got, dp_index // ratio, 0, keepdims=False)[..., out_width:]
    share = jnp.concatenate([total, piece], axis=-1)
    everyone = lax.all_to_all(
        jnp.broadcast_to(share, (n_tensor,) + share.shape), PLANE, 0, 0, tiled=True
    )
    near = everyone[:, 0].reshape(rows, out_width + block_width)
    far = everyone[:, 1].reshape(rows, out_width + block_width)

    def gram(gate, columns):
        return lax.dot_general(
            gate, columns, (((0,), (0,)), ((), ())), preferred_element_type=jnp.float32
        )

    gram_tile = gram(gate_near, near[:, out_width:]) + gram(gate_far, far[:, out_width:])
    factor = prior_factor.astype(jnp.float32) + gram_tile / (2 * rows)
    near, far = near[:, :out_width], far[:, :out_width]
    first, second = jnp.where(cross == 0, near, far), jnp.where(cross == 0, far, near)
    return jnp.concatenate([first, second]), factor


def solution(mesh):
    split = Mesh(mesh.devices.reshape(2, 16, 2, 4, 2), ("xh",) + LINE + PLANE)
    dp, tensor = ("xh",) + LINE, PLANE
    return jax.shard_map(
        shards,
        mesh=split,
        in_specs=(P(dp, tensor),) * 5 + (P(tensor, dp),),
        out_specs=(P(None, dp), P(tensor, dp)),
        check_vma=False,
    )
```

```python
import jax
import jax.numpy as jnp
from jax import lax
from jax.experimental.layout import Layout, with_layout_constraint
from jax.sharding import Mesh, PartitionSpec as P

PLANE = ("y", "xl")
LINE = ("z", "c")
STEPS = 15


def derivatives(incoming_raw, gate_raw, upper_raw):
    gate_val = gate_raw.astype(jnp.float32)
    upper_val = upper_raw.astype(jnp.float32)
    incoming = incoming_raw.astype(jnp.float32)
    sigmoid_val = jax.nn.sigmoid(gate_val)
    gate_grad = incoming * upper_val * sigmoid_val * (1.0 + gate_val * (1.0 - sigmoid_val))
    upper_grad = incoming * gate_val * sigmoid_val
    return (
        lax.reduce_precision(gate_grad, 8, 7),
        lax.reduce_precision(upper_grad, 8, 7),
    )


def ladder(values):
    largest = jnp.max(jnp.abs(values), axis=1, keepdims=True)
    place = jnp.zeros_like(largest)
    scale = jnp.full_like(largest, 2.0**9)
    for step in range(1, STEPS):
        below = largest <= 2.0 ** (6 - 8 * step)
        place = jnp.where(below, float(step), place)
        scale = jnp.where(below, 2.0 ** (9 + 8 * step), scale)
    return scale, place


def unladder(values, place):
    place = place.astype(jnp.float32)
    undo = jnp.full_like(place, 2.0**-9)
    for step in range(1, STEPS):
        undo = jnp.where(place == float(step), 2.0 ** -(9 + 8 * step), undo)
    return (values.astype(jnp.float32) * undo).astype(jnp.bfloat16)


def by_rows(block):
    return with_layout_constraint(block, Layout(major_to_minor=(0, 1)))


def swap(block):
    return lax.ppermute(block, "xh", [(0, 1), (1, 0)])


def lender_slot(cross, z, column):
    return 4 * cross + (z // 4 - column % 4 + z % 4) % 4


def lend(block):
    pairs = []
    for cross in range(2):
        for z in range(16):
            for core in range(2):
                for column in range(8):
                    to_z = 4 * (column % 4) + z % 4
                    to_line = (column // 4 * 16 + to_z) * 2 + core
                    to_place = lender_slot(cross, z, column)
                    pairs.append(
                        (((cross * 16 + z) * 2 + core) * 8 + column, to_line * 8 + to_place)
                    )
    return lax.ppermute(block, ("xh",) + LINE + PLANE, pairs)


def product(tokens, weight):
    return lax.dot_general(
        tokens, weight, (((1,), (1,)), ((), ())), preferred_element_type=jnp.float32
    )


def shards(grad_hidden, gate_in, up_in, gate_weight, up_weight, prior_factor):
    held, width = grad_hidden.shape
    block_width = prior_factor.shape[1]
    out_width = gate_weight.shape[0]
    n_tensor = lax.axis_size(PLANE)
    dp_index = lax.axis_index(("xh",) + LINE)
    cross, ratio = lax.axis_index("xh"), width // block_width

    gate_grad, upper_grad = derivatives(grad_hidden, gate_in, up_in)
    far_grad = swap(gate_grad.astype(jnp.bfloat16))
    up_both = jnp.concatenate([up_weight, swap(up_weight)])
    far_grad = far_grad.astype(jnp.float32)
    scale, place = ladder(jnp.concatenate([gate_grad, upper_grad], axis=1))
    far_scale, far_place = ladder(far_grad)
    lanes = lax.broadcasted_iota(jnp.int32, (held, 128), 1)
    packed = jnp.concatenate(
        [gate_grad * scale, upper_grad * scale, far_grad * far_scale]
        + [jnp.where(lanes < 64, place, far_place)],
        axis=1,
    ).astype(jnp.float16)
    packed = lax.all_gather(packed, LINE, axis=0, tiled=True)
    place, far_place = packed[:, 3 * width : 3 * width + 1], packed[:, -1:]
    upper_near = unladder(packed[:, width : 2 * width], place)
    gate_near = by_rows(unladder(packed[:, :width], place))
    gate_far = by_rows(unladder(packed[:, 2 * width : 3 * width], far_place))
    upper_near, gate_near, gate_far = lax.optimization_barrier((upper_near, gate_near, gate_far))
    rows = gate_near.shape[0]
    slot = rows // n_tensor

    column = lax.axis_index(PLANE)
    to_slot = lender_slot(cross, lax.axis_index("z"), column)

    def cut(gate):
        start = (to_slot * slot, dp_index % ratio * block_width)
        return lax.dynamic_slice(gate, start, (slot, block_width))

    ours, theirs = cut(gate_near), cut(gate_far)
    same_side = column // 4 == cross
    piece = lend(
        jnp.stack([jnp.where(same_side, ours, theirs), jnp.where(same_side, theirs, ours)])
    )

    upper_sum = product(upper_near, up_both)
    upper_sum, gate_near, gate_far = lax.optimization_barrier((upper_sum, gate_near, gate_far))
    far_sum = swap(upper_sum[:, out_width:].astype(jnp.bfloat16)).astype(jnp.float32)
    far_sum, piece = lax.optimization_barrier((far_sum, piece))

    def part(gate, upper_sum):
        sums = (product(gate, gate_weight) + upper_sum).astype(jnp.bfloat16)
        return sums.reshape(n_tensor, 1, slot, out_width)

    sent = jnp.concatenate(
        [part(gate_near, upper_sum[:, :out_width]), part(gate_far, far_sum)], axis=1
    )
    got = lax.all_to_all(sent, PLANE, 0, 0, tiled=True)
    total = jnp.sum(got.astype(jnp.float32), axis=0).astype(jnp.bfloat16)
    share = jnp.concatenate([total, piece], axis=-1)
    everyone = lax.all_to_all(
        jnp.broadcast_to(share, (n_tensor,) + share.shape), PLANE, 0, 0, tiled=True
    )
    near = everyone[:, 0].reshape(rows, out_width + block_width)
    far = everyone[:, 1].reshape(rows, out_width + block_width)

    def gram(gate, columns):
        return lax.dot_general(
            gate, columns, (((0,), (0,)), ((), ())), preferred_element_type=jnp.float32
        )

    gram_tile = gram(gate_near, near[:, out_width:]) + gram(gate_far, far[:, out_width:])
    factor = prior_factor.astype(jnp.float32) + gram_tile / (2 * rows)
    near, far = near[:, :out_width], far[:, :out_width]
    first, second = jnp.where(cross == 0, near, far), jnp.where(cross == 0, far, near)
    return jnp.concatenate([first, second]), factor


def solution(mesh):
    split = Mesh(mesh.devices.reshape(2, 16, 2, 4, 2), ("xh",) + LINE + PLANE)
    dp, tensor = ("xh",) + LINE, PLANE
    return jax.shard_map(
        shards,
        mesh=split,
        in_specs=(P(dp, tensor),) * 5 + (P(tensor, dp),),
        out_specs=(P(None, dp), P(tensor, dp)),
        check_vma=False,
    )
```

```python
import jax
import jax.numpy as jnp
from jax import lax
from jax.experimental.layout import Layout, with_layout_constraint
from jax.sharding import Mesh, PartitionSpec as P

PLANE = ("y", "xl")
LINE = ("z", "c")
STEPS = 15


def derivatives(incoming_raw, gate_raw, upper_raw):
    gate_val = gate_raw.astype(jnp.float32)
    upper_val = upper_raw.astype(jnp.float32)
    incoming = incoming_raw.astype(jnp.float32)
    sigmoid_val = jax.nn.sigmoid(gate_val)
    gate_grad = incoming * upper_val * sigmoid_val * (1.0 + gate_val * (1.0 - sigmoid_val))
    upper_grad = incoming * gate_val * sigmoid_val
    return (
        lax.reduce_precision(gate_grad, 8, 7),
        lax.reduce_precision(upper_grad, 8, 7),
    )


def ladder(values):
    largest = jnp.max(jnp.abs(values), axis=1, keepdims=True)
    place = jnp.zeros_like(largest)
    scale = jnp.full_like(largest, 2.0**9)
    for step in range(1, STEPS):
        below = largest <= 2.0 ** (6 - 8 * step)
        place = jnp.where(below, float(step), place)
        scale = jnp.where(below, 2.0 ** (9 + 8 * step), scale)
    return scale, place


def unladder(values, place):
    place = place.astype(jnp.float32)
    undo = jnp.full_like(place, 2.0**-9)
    for step in range(1, STEPS):
        undo = jnp.where(place == float(step), 2.0 ** -(9 + 8 * step), undo)
    return (values.astype(jnp.float32) * undo).astype(jnp.bfloat16)


def by_rows(block):
    return with_layout_constraint(block, Layout(major_to_minor=(0, 1)))


def swap(block):
    return lax.ppermute(block, "xh", [(0, 1), (1, 0)])


def product(tokens, weight):
    return lax.dot_general(
        tokens, weight, (((1,), (1,)), ((), ())), preferred_element_type=jnp.float32
    )


def shards(grad_hidden, gate_in, up_in, gate_weight, up_weight, prior_factor):
    held, width = grad_hidden.shape
    block_width = prior_factor.shape[1]
    out_width = gate_weight.shape[0]
    n_tensor = lax.axis_size(PLANE)
    dp_index = lax.axis_index(("xh",) + LINE)
    cross, ratio = lax.axis_index("xh"), width // block_width

    gate_grad, upper_grad = derivatives(grad_hidden, gate_in, up_in)
    far_grad = swap(gate_grad.astype(jnp.bfloat16))
    up_both = jnp.concatenate([up_weight, swap(up_weight)])
    far_grad = far_grad.astype(jnp.float32)
    scale, place = ladder(jnp.concatenate([gate_grad, upper_grad], axis=1))
    far_scale, far_place = ladder(far_grad)
    lanes = lax.broadcasted_iota(jnp.int32, (held, 128), 1)
    packed = jnp.concatenate(
        [gate_grad * scale, upper_grad * scale, far_grad * far_scale]
        + [jnp.where(lanes < 64, place, far_place)],
        axis=1,
    ).astype(jnp.float16)
    packed = lax.all_gather(packed, LINE, axis=0, tiled=True)
    place, far_place = packed[:, 3 * width : 3 * width + 1], packed[:, -1:]
    upper_near = unladder(packed[:, width : 2 * width], place)
    gate_near = by_rows(unladder(packed[:, :width], place))
    gate_far = by_rows(unladder(packed[:, 2 * width : 3 * width], far_place))
    rows = gate_near.shape[0]
    slot = rows // n_tensor

    upper_sum = product(upper_near, up_both)
    upper_sum, gate_near, gate_far = lax.optimization_barrier((upper_sum, gate_near, gate_far))
    far_sum = swap(upper_sum[:, out_width:].astype(jnp.bfloat16)).astype(jnp.float32)

    def part(gate, upper_sum):
        sums = (product(gate, gate_weight) + upper_sum).astype(jnp.bfloat16)
        cut = lax.dynamic_slice_in_dim(gate, dp_index % ratio * block_width, block_width, 1)
        return jnp.concatenate([sums, cut], axis=1).reshape(n_tensor, 1, slot, -1)

    sent = jnp.concatenate(
        [part(gate_near, upper_sum[:, :out_width]), part(gate_far, far_sum)], axis=1
    )
    got = lax.all_to_all(sent, PLANE, 0, 0, tiled=True)
    total = jnp.sum(got[..., :out_width].astype(jnp.float32), axis=0).astype(jnp.bfloat16)
    piece = lax.dynamic_index_in_dim(got, dp_index // ratio, 0, keepdims=False)[..., out_width:]
    share = jnp.concatenate([total, piece], axis=-1)
    everyone = lax.all_to_all(
        jnp.broadcast_to(share, (n_tensor,) + share.shape), PLANE, 0, 0, tiled=True
    )
    near = everyone[:, 0].reshape(rows, out_width + block_width)
    far = everyone[:, 1].reshape(rows, out_width + block_width)

    def gram(gate, columns):
        return lax.dot_general(
            gate, columns, (((0,), (0,)), ((), ())), preferred_element_type=jnp.float32
        )

    gram_tile = gram(gate_near, near[:, out_width:]) + gram(gate_far, far[:, out_width:])
    factor = prior_factor.astype(jnp.float32) + gram_tile / (2 * rows)
    near, far = near[:, :out_width], far[:, :out_width]
    first, second = jnp.where(cross == 0, near, far), jnp.where(cross == 0, far, near)
    return jnp.concatenate([first, second]), factor


def solution(mesh):
    split = Mesh(mesh.devices.reshape(2, 16, 2, 4, 2), ("xh",) + LINE + PLANE)
    dp, tensor = ("xh",) + LINE, PLANE
    return jax.shard_map(
        shards,
        mesh=split,
        in_specs=(P(dp, tensor),) * 5 + (P(tensor, dp),),
        out_specs=(P(None, dp), P(tensor, dp)),
        check_vma=False,
    )
```

```python
import jax
import jax.numpy as jnp
from jax import lax
from jax.experimental.layout import Layout, with_layout_constraint
from jax.sharding import Mesh, PartitionSpec as P

PLANE = ("y", "xl")
LINE = ("z", "c")
STEPS = 15


def derivatives(incoming_raw, gate_raw, upper_raw):
    gate_val = gate_raw.astype(jnp.float32)
    upper_val = upper_raw.astype(jnp.float32)
    incoming = incoming_raw.astype(jnp.float32)
    sigmoid_val = jax.nn.sigmoid(gate_val)
    gate_grad = incoming * upper_val * sigmoid_val * (1.0 + gate_val * (1.0 - sigmoid_val))
    upper_grad = incoming * gate_val * sigmoid_val
    return (
        lax.reduce_precision(gate_grad, 8, 7),
        lax.reduce_precision(upper_grad, 8, 7),
    )


def ladder(values):
    largest = jnp.max(jnp.abs(values), axis=1, keepdims=True)
    place = jnp.zeros_like(largest)
    scale = jnp.full_like(largest, 2.0**9)
    for step in range(1, STEPS):
        below = largest <= 2.0 ** (6 - 8 * step)
        place = jnp.where(below, float(step), place)
        scale = jnp.where(below, 2.0 ** (9 + 8 * step), scale)
    return scale, place


def unladder(values, place):
    place = place.astype(jnp.float32)
    undo = jnp.full_like(place, 2.0**-9)
    for step in range(1, STEPS):
        undo = jnp.where(place == float(step), 2.0 ** -(9 + 8 * step), undo)
    return (values.astype(jnp.float32) * undo).astype(jnp.bfloat16)


def by_rows(block):
    return with_layout_constraint(block, Layout(major_to_minor=(0, 1)))


def swap(block):
    return lax.ppermute(block, "xh", [(0, 1), (1, 0)])


def product(tokens, weight):
    return lax.dot_general(
        tokens, weight, (((1,), (1,)), ((), ())), preferred_element_type=jnp.float32
    )


def shards(grad_hidden, gate_in, up_in, gate_weight, up_weight, prior_factor):
    held, width = grad_hidden.shape
    block_width = prior_factor.shape[1]
    out_width = gate_weight.shape[0]
    n_tensor = lax.axis_size(PLANE)
    dp_index = lax.axis_index(("xh",) + LINE)
    cross, ratio = lax.axis_index("xh"), width // block_width

    gate_grad, upper_grad = derivatives(grad_hidden, gate_in, up_in)
    far_grad = swap(gate_grad.astype(jnp.bfloat16))
    up_both = jnp.concatenate([up_weight, swap(up_weight)])
    far_grad = far_grad.astype(jnp.float32)
    scale, place = ladder(jnp.concatenate([gate_grad, upper_grad], axis=1))
    far_scale, far_place = ladder(far_grad)
    lanes = lax.broadcasted_iota(jnp.int32, (held, 128), 1)
    packed = jnp.concatenate(
        [gate_grad * scale, upper_grad * scale, far_grad * far_scale]
        + [jnp.where(lanes < 64, place, far_place)],
        axis=1,
    ).astype(jnp.float16)
    packed = lax.all_gather(packed, LINE, axis=0, tiled=True)
    place, far_place = packed[:, 3 * width : 3 * width + 1], packed[:, -1:]
    upper_near = unladder(packed[:, width : 2 * width], place)
    gate_near = by_rows(unladder(packed[:, :width], place))
    gate_far = by_rows(unladder(packed[:, 2 * width : 3 * width], far_place))
    upper_near, gate_near, gate_far = lax.optimization_barrier((upper_near, gate_near, gate_far))
    rows = gate_near.shape[0]
    slot = rows // n_tensor

    def cut(gate):
        columns = dp_index % ratio * block_width
        return lax.dynamic_slice_in_dim(gate, columns, block_width, 1).reshape(
            n_tensor, 1, slot, block_width
        )

    pieces = lax.all_to_all(
        jnp.concatenate([cut(gate_near), cut(gate_far)], axis=1), PLANE, 0, 0, tiled=True
    )
    piece = lax.dynamic_index_in_dim(pieces, dp_index // ratio, 0, keepdims=False)

    upper_sum = product(upper_near, up_both)
    upper_sum, gate_near, gate_far = lax.optimization_barrier((upper_sum, gate_near, gate_far))
    far_sum = swap(upper_sum[:, out_width:].astype(jnp.bfloat16)).astype(jnp.float32)
    far_sum, piece = lax.optimization_barrier((far_sum, piece))

    def part(gate, upper_sum):
        sums = (product(gate, gate_weight) + upper_sum).astype(jnp.bfloat16)
        return sums.reshape(n_tensor, 1, slot, out_width)

    sent = jnp.concatenate(
        [part(gate_near, upper_sum[:, :out_width]), part(gate_far, far_sum)], axis=1
    )
    got = lax.all_to_all(sent, PLANE, 0, 0, tiled=True)
    total = jnp.sum(got.astype(jnp.float32), axis=0).astype(jnp.bfloat16)
    share = jnp.concatenate([total, piece], axis=-1)
    everyone = lax.all_to_all(
        jnp.broadcast_to(share, (n_tensor,) + share.shape), PLANE, 0, 0, tiled=True
    )
    near = everyone[:, 0].reshape(rows, out_width + block_width)
    far = everyone[:, 1].reshape(rows, out_width + block_width)

    def gram(gate, columns):
        return lax.dot_general(
            gate, columns, (((0,), (0,)), ((), ())), preferred_element_type=jnp.float32
        )

    gram_tile = gram(gate_near, near[:, out_width:]) + gram(gate_far, far[:, out_width:])
    factor = prior_factor.astype(jnp.float32) + gram_tile / (2 * rows)
    near, far = near[:, :out_width], far[:, :out_width]
    first, second = jnp.where(cross == 0, near, far), jnp.where(cross == 0, far, near)
    return jnp.concatenate([first, second]), factor


def solution(mesh):
    split = Mesh(mesh.devices.reshape(2, 16, 2, 4, 2), ("xh",) + LINE + PLANE)
    dp, tensor = ("xh",) + LINE, PLANE
    return jax.shard_map(
        shards,
        mesh=split,
        in_specs=(P(dp, tensor),) * 5 + (P(tensor, dp),),
        out_specs=(P(None, dp), P(tensor, dp)),
        check_vma=False,
    )
```

```python
import jax
import jax.numpy as jnp
from jax import lax
from jax.experimental.layout import Layout, with_layout_constraint
from jax.sharding import Mesh, PartitionSpec as P

PLANE = ("y", "xl")
LINE = ("z", "c")
STEPS = 15


def derivatives(incoming_raw, gate_raw, upper_raw):
    gate_val = gate_raw.astype(jnp.float32)
    upper_val = upper_raw.astype(jnp.float32)
    incoming = incoming_raw.astype(jnp.float32)
    sigmoid_val = jax.nn.sigmoid(gate_val)
    gate_grad = incoming * upper_val * sigmoid_val * (1.0 + gate_val * (1.0 - sigmoid_val))
    upper_grad = incoming * gate_val * sigmoid_val
    return (
        lax.reduce_precision(gate_grad, 8, 7),
        lax.reduce_precision(upper_grad, 8, 7),
    )


def ladder(values):
    largest = jnp.max(jnp.abs(values), axis=1, keepdims=True)
    place = jnp.zeros_like(largest)
    scale = jnp.full_like(largest, 2.0**9)
    for step in range(1, STEPS):
        below = largest <= 2.0 ** (6 - 8 * step)
        place = jnp.where(below, float(step), place)
        scale = jnp.where(below, 2.0 ** (9 + 8 * step), scale)
    return scale, place


def unladder(values, place):
    place = place.astype(jnp.float32)
    undo = jnp.full_like(place, 2.0**-9)
    for step in range(1, STEPS):
        undo = jnp.where(place == float(step), 2.0 ** -(9 + 8 * step), undo)
    return (values.astype(jnp.float32) * undo).astype(jnp.bfloat16)


def by_rows(block):
    return with_layout_constraint(block, Layout(major_to_minor=(0, 1)))


def swap(block):
    return lax.ppermute(block, "xh", [(0, 1), (1, 0)])


def product(tokens, weight):
    return lax.dot_general(
        tokens, weight, (((1,), (1,)), ((), ())), preferred_element_type=jnp.float32
    )


def shards(grad_hidden, gate_in, up_in, gate_weight, up_weight, prior_factor):
    held, width = grad_hidden.shape
    block_width = prior_factor.shape[1]
    out_width = gate_weight.shape[0]
    n_tensor = lax.axis_size(PLANE)
    dp_index = lax.axis_index(("xh",) + LINE)
    cross, ratio = lax.axis_index("xh"), width // block_width

    gate_grad, upper_grad = derivatives(grad_hidden, gate_in, up_in)
    far_grad = swap(gate_grad.astype(jnp.bfloat16))
    gate_both = jnp.concatenate([gate_weight, swap(gate_weight)])
    up_both = jnp.concatenate([up_weight, swap(up_weight)])
    far_grad = far_grad.astype(jnp.float32)
    scale, place = ladder(jnp.concatenate([gate_grad, upper_grad], axis=1))
    far_scale, far_place = ladder(far_grad)
    lanes = lax.broadcasted_iota(jnp.int32, (held, 128), 1)
    packed = jnp.concatenate(
        [gate_grad * scale, upper_grad * scale, far_grad * far_scale]
        + [jnp.where(lanes < 64, place, far_place)],
        axis=1,
    ).astype(jnp.float16)
    packed = lax.all_gather(packed, LINE, axis=0, tiled=True)
    place, far_place = packed[:, 3 * width : 3 * width + 1], packed[:, -1:]
    upper_near = unladder(packed[:, width : 2 * width], place)
    gate_near = by_rows(unladder(packed[:, :width], place))
    gate_far = by_rows(unladder(packed[:, 2 * width : 3 * width], far_place))
    upper_near, gate_near, gate_far = lax.optimization_barrier((upper_near, gate_near, gate_far))
    rows = gate_near.shape[0]
    slot = rows // n_tensor

    sums = (product(gate_near, gate_both) + product(upper_near, up_both)).astype(jnp.bfloat16)
    ours, theirs = sums[:, :out_width], sums[:, out_width:]
    cut = lax.dynamic_slice_in_dim(gate_near, dp_index % ratio * block_width, block_width, 1)

    def slots(sums):
        return jnp.concatenate([sums, cut], axis=1).reshape(n_tensor, slot, -1)

    sent = jnp.concatenate(
        [slots(jnp.where(cross == 0, ours, theirs)), slots(jnp.where(cross == 0, theirs, ours))]
    )
    got = lax.all_to_all(sent, ("xh",) + PLANE, 0, 0, tiled=True)
    got = got.reshape(2, n_tensor, slot, out_width + block_width)
    total = jnp.sum(got[..., :out_width].astype(jnp.float32), axis=1).astype(jnp.bfloat16)
    piece = lax.dynamic_index_in_dim(got, dp_index // ratio, 1, keepdims=False)[..., out_width:]
    share = jnp.concatenate([total, piece], axis=-1)
    everyone = lax.all_to_all(
        jnp.broadcast_to(share, (n_tensor,) + share.shape), PLANE, 0, 0, tiled=True
    )
    first = everyone[:, 0].reshape(rows, out_width + block_width)
    second = everyone[:, 1].reshape(rows, out_width + block_width)

    def gram(gate, columns):
        return lax.dot_general(
            gate, columns, (((0,), (0,)), ((), ())), preferred_element_type=jnp.float32
        )

    first_cols, second_cols = first[:, out_width:], second[:, out_width:]
    near_cols = jnp.where(cross == 0, first_cols, second_cols)
    far_cols = jnp.where(cross == 0, second_cols, first_cols)
    gram_tile = gram(gate_near, near_cols) + gram(gate_far, far_cols)
    factor = prior_factor.astype(jnp.float32) + gram_tile / (2 * rows)
    return jnp.concatenate([first[:, :out_width], second[:, :out_width]]), factor


def solution(mesh):
    split = Mesh(mesh.devices.reshape(2, 16, 2, 4, 2), ("xh",) + LINE + PLANE)
    dp, tensor = ("xh",) + LINE, PLANE
    return jax.shard_map(
        shards,
        mesh=split,
        in_specs=(P(dp, tensor),) * 5 + (P(tensor, dp),),
        out_specs=(P(None, dp), P(tensor, dp)),
        check_vma=False,
    )
```

```python
import jax
import jax.numpy as jnp
from jax import lax
from jax.experimental.layout import Layout, with_layout_constraint
from jax.sharding import Mesh, PartitionSpec as P

PLANE = ("y", "xl")
LINE = ("z", "c")
STEPS = 15


def derivatives(incoming_raw, gate_raw, upper_raw):
    gate_val = gate_raw.astype(jnp.float32)
    upper_val = upper_raw.astype(jnp.float32)
    incoming = incoming_raw.astype(jnp.float32)
    sigmoid_val = jax.nn.sigmoid(gate_val)
    gate_grad = incoming * upper_val * sigmoid_val * (1.0 + gate_val * (1.0 - sigmoid_val))
    upper_grad = incoming * gate_val * sigmoid_val
    return (
        lax.reduce_precision(gate_grad, 8, 7),
        lax.reduce_precision(upper_grad, 8, 7),
    )


def ladder(values):
    largest = jnp.max(jnp.abs(values), axis=1, keepdims=True)
    place = jnp.zeros_like(largest)
    scale = jnp.full_like(largest, 2.0**9)
    for step in range(1, STEPS):
        below = largest <= 2.0 ** (6 - 8 * step)
        place = jnp.where(below, float(step), place)
        scale = jnp.where(below, 2.0 ** (9 + 8 * step), scale)
    return scale, place


def unladder(values, place):
    place = place.astype(jnp.float32)
    undo = jnp.full_like(place, 2.0**-9)
    for step in range(1, STEPS):
        undo = jnp.where(place == float(step), 2.0 ** -(9 + 8 * step), undo)
    return (values.astype(jnp.float32) * undo).astype(jnp.bfloat16)


def by_rows(block):
    return with_layout_constraint(block, Layout(major_to_minor=(0, 1)))


def swap(block):
    return lax.ppermute(block, "xh", [(0, 1), (1, 0)])


def product(tokens, weight):
    return lax.dot_general(
        tokens, weight, (((1,), (1,)), ((), ())), preferred_element_type=jnp.float32
    )


def shards(grad_hidden, gate_in, up_in, gate_weight, up_weight, prior_factor):
    held, width = grad_hidden.shape
    block_width = prior_factor.shape[1]
    out_width = gate_weight.shape[0]
    n_tensor = lax.axis_size(PLANE)
    dp_index = lax.axis_index(("xh",) + LINE)
    cross, ratio = lax.axis_index("xh"), width // block_width

    gate_grad, upper_grad = derivatives(grad_hidden, gate_in, up_in)
    gate_both = jnp.concatenate([gate_weight, swap(gate_weight)])
    up_both = jnp.concatenate([up_weight, swap(up_weight)])
    scale, place = ladder(jnp.concatenate([gate_grad, upper_grad], axis=1))
    tail = jnp.broadcast_to(place, (held, 128))
    packed = jnp.concatenate([gate_grad * scale, upper_grad * scale, tail], axis=1)
    packed = packed.astype(jnp.float16)
    packed = lax.all_gather(packed, LINE, axis=0, tiled=True)
    place = packed[:, 2 * width : 2 * width + 1]
    upper_near = unladder(packed[:, width : 2 * width], place)
    gate_near = by_rows(unladder(packed[:, :width], place))
    upper_near, gate_near = lax.optimization_barrier((upper_near, gate_near))
    rows = gate_near.shape[0]
    slot, core, half = rows // n_tensor, lax.axis_index("c"), rows // 2

    far_mine = by_rows(swap(lax.dynamic_slice_in_dim(gate_near, core * half, half, 0)))
    far_other = by_rows(lax.ppermute(far_mine, "c", [(0, 1), (1, 0)]))

    sums = (product(gate_near, gate_both) + product(upper_near, up_both)).astype(jnp.bfloat16)
    ours, theirs = sums[:, :out_width], sums[:, out_width:]
    cut = lax.dynamic_slice_in_dim(gate_near, dp_index % ratio * block_width, block_width, 1)

    def slots(sums):
        return jnp.concatenate([sums, cut], axis=1).reshape(n_tensor, slot, -1)

    sent = jnp.concatenate(
        [slots(jnp.where(cross == 0, ours, theirs)), slots(jnp.where(cross == 0, theirs, ours))]
    )
    got = lax.all_to_all(sent, ("xh",) + PLANE, 0, 0, tiled=True)
    got = got.reshape(2, n_tensor, slot, out_width + block_width)
    total = jnp.sum(got[..., :out_width].astype(jnp.float32), axis=1).astype(jnp.bfloat16)
    piece = lax.dynamic_index_in_dim(got, dp_index // ratio, 1, keepdims=False)[..., out_width:]
    share = jnp.concatenate([total, piece], axis=-1)
    everyone = lax.all_to_all(
        jnp.broadcast_to(share, (n_tensor,) + share.shape), PLANE, 0, 0, tiled=True
    )
    first = everyone[:, 0].reshape(rows, out_width + block_width)
    second = everyone[:, 1].reshape(rows, out_width + block_width)

    def gram(gate, columns):
        return lax.dot_general(
            gate, columns, (((0,), (0,)), ((), ())), preferred_element_type=jnp.float32
        )

    first_cols, second_cols = first[:, out_width:], second[:, out_width:]
    near_cols = jnp.where(cross == 0, first_cols, second_cols)
    far_cols = jnp.where(cross == 0, second_cols, first_cols)
    far_cols = far_cols.reshape(2, half, block_width)
    gram_tile = (
        gram(gate_near, near_cols)
        + gram(far_mine, lax.dynamic_index_in_dim(far_cols, core, 0, keepdims=False))
        + gram(far_other, lax.dynamic_index_in_dim(far_cols, 1 - core, 0, keepdims=False))
    )
    factor = prior_factor.astype(jnp.float32) + gram_tile / (2 * rows)
    return jnp.concatenate([first[:, :out_width], second[:, :out_width]]), factor


def solution(mesh):
    split = Mesh(mesh.devices.reshape(2, 16, 2, 4, 2), ("xh",) + LINE + PLANE)
    dp, tensor = ("xh",) + LINE, PLANE
    return jax.shard_map(
        shards,
        mesh=split,
        in_specs=(P(dp, tensor),) * 5 + (P(tensor, dp),),
        out_specs=(P(None, dp), P(tensor, dp)),
        check_vma=False,
    )
```
